512 devices in a mesh: wide: 64 (over x, z_lo, core), node: 8 (over z_hi, y).
Axes of the slice: x: 4, y: 4, z: 16 (z_hi: 2, z_lo: 8; z = z_hi * 8 + z_lo), core: 2. Of those that a mesh axis runs over, the one named last changes fastest.
Arguments:
- hidden: bfloat16 [8192, 24576], P('node', 'wide'), may hold values from -6 to 6
- cotangent: bfloat16 [8192, 4096], P(('node', 'wide')), may hold values from -6 to 6
- weight_codes: bfloat16 [4096, 24576], P('node', 'wide'), may hold values from -0.0390625 to 0.0390625
- block_scales: bfloat16 [32, 24576], P('node', 'wide'), may hold values from 0.25 to 4
Outputs:
- hidden_grad: bfloat16 [8192, 24576], P('node', 'wide')
- weight_grad: bfloat16 [4096, 24576], P('node', 'wide')
The draws below stay inside these ranges and needn't reach their ends.
All inputs are finite; a program needn't handle non-finite values.
Results may differ from the reference program's by a relative error of at most 0.015.
Values may be sent and summed in bfloat16 or wider, within the bound.
A program may use at most 64 MiB of HBM per device.

```python
import math
import jax
import jax.numpy as jnp

D = 4096
FB = 384
QBLOCK = 128
TOK_DEV = 1024
FF = 24576
TOKENS = 8192
N_WIDE = 64
N_NODE = 8


def shard_levels(own_key, dims, cuts, least, high):
    level = 1.0
    for position, blocks in cuts:
        draws = jax.random.uniform(jax.random.fold_in(jax.random.fold_in(own_key, 6), position), (blocks,), jnp.float32, least / len(cuts), high / len(cuts))
        level = level * jnp.repeat(jnp.exp(draws), dims[position] // blocks).reshape((-1,) + (1,) * (len(dims) - 1 - position))
    return level


def normal_values(stream_key, dims, spread, bound, pieces=(), dtype=jnp.bfloat16):
    entries = spread * jax.random.normal(stream_key, dims, jnp.float32)
    if pieces:
        entries = entries * shard_levels(stream_key, dims, pieces, -0.22, 0.18)
    return jnp.clip(entries, -bound, bound).astype(dtype)


def setup_inputs(seed: int = 0) -> dict:
    key_of = jax.random.split(jax.random.key(seed), 5)
    return {
        "hidden": normal_values(key_of[0], (TOKENS, FF), 1.0, 6.0, ((0, 8), (1, 64))),
        "cotangent": normal_values(key_of[1], (TOKENS, D), 1.0, 6.0, ((0, 512),)),
        "weight_codes": normal_values(key_of[2], (D, FF), FF ** -0.5, 0.0390625, ((0, 8), (1, 64))),
        "block_scales": jnp.clip(jnp.exp(math.log(4.0) - 2.7725887 * jax.random.uniform(key_of[3], (D // QBLOCK, FF), jnp.float32) ** shard_levels(key_of[3], (D // QBLOCK, FF), ((0, 8), (1, 64)), -0.2, 0.2)), 0.25, 4.0).astype(jnp.bfloat16),
    }


def reference(hidden, cotangent, weight_codes, block_scales):
    codes = weight_codes.astype(jnp.float32).reshape(D // QBLOCK, QBLOCK, FB * N_WIDE)
    weight = (codes * block_scales.astype(jnp.float32)[:, None, :]).reshape(D, FB * N_WIDE).astype(jnp.bfloat16)
    hidden_grad = jnp.dot(cotangent, weight, preferred_element_type=jnp.float32).astype(jnp.bfloat16)
    grad_scale = (TOK_DEV * N_NODE) ** -0.5
    total = jnp.zeros((D, FB * N_WIDE), jnp.float32)
    for group in range(N_NODE):
        rows_cot = cotangent[group * TOK_DEV:(group + 1) * TOK_DEV]
        rows_hid = hidden[group * TOK_DEV:(group + 1) * TOK_DEV]
        partial_term = grad_scale * jnp.dot(rows_cot.T, rows_hid, preferred_element_type=jnp.float32)
        total = total + partial_term.astype(jnp.bfloat16).astype(jnp.float32)
    return hidden_grad, total.astype(jnp.bfloat16)
```

```python
import functools

import jax
import jax.numpy as jnp
from jax import lax
from jax.experimental import pallas as pl
from jax.experimental.pallas import tpu as pltpu
from jax.sharding import PartitionSpec as P

MESH = pl.DeviceIdType.MESH
NX, NY, NZ = 4, 4, 8
D, FB, TOK, ROWS, QB = 4096, 384, 1024, 16, 128
OWN = D // 8
HALF = D // 2
FZ = 2
F32, BF16 = jnp.float32, jnp.bfloat16


def kernel(
    hid_hbm, cot_hbm, codes_hbm, scales_ref,
    hgrad_ref, wgrad_ref,
    cot, hid, hid_t, codes, weight, part, ywhole, yhalf, zsum, zgot, near_sum, hacc,
    local_sem, z_s, z_r, x_s, x_r, xh_s, xh_r, c_s, c_r,
    wy_s, wy_r, wh_s, wh_r, wz_s, wz_r, gy_s, gy_r, gh_s, gh_r, gz_s, gz_r,
):
    wide, node = lax.axis_index("wide"), lax.axis_index("node")
    x, zl, core = wide // (2 * NZ), (wide // 2) % NZ, wide % 2
    zh, y = node // NY, node % NY

    def at(dx=0, dy=0, dz=0):
        z = (zh * NZ + zl + dz + 2 * NZ) % (2 * NZ)
        return (
            ((x + dx + NX) % NX) * 2 * NZ + (z % NZ) * 2 + core,
            (z // NZ) * NY + (y + dy + NY) % NY,
        )

    sibling = (wide + 1 - 2 * core, node)
    right_of = {"x": at(dx=1), "y": at(dy=1), "z": at(dz=1)}
    left_of = {"x": at(dx=-1), "y": at(dy=-1), "z": at(dz=-1)}
    across = at(dz=NZ)
    sent = []

    def remote(src, dst, s, r, to):
        return pltpu.make_async_remote_copy(
            src_ref=src, dst_ref=dst, send_sem=s, recv_sem=r, device_id=to, device_id_type=MESH
        )

    def send(src, dst, s, r, to):
        copy = remote(src, dst, s, r, to)
        copy.start()
        sent.append((None, copy))

    def landed(dst, r):
        remote(dst, dst, r, r, sibling).wait_recv()

    barrier = pltpu.get_barrier_semaphore()
    peers = [*right_of.values(), *left_of.values(), sibling, across]
    for peer in peers:
        pl.semaphore_signal(barrier, inc=1, device_id=peer, device_id_type=MESH)
    loads = [
        pltpu.make_async_copy(cot_hbm, cot.at[wide], local_sem.at[0]),
        pltpu.make_async_copy(codes_hbm, codes, local_sem.at[1]),
        pltpu.make_async_copy(hid_hbm, hid, local_sem.at[2]),
    ]
    for load in loads:
        load.start()
    loads[0].wait()
    pl.semaphore_wait(barrier, len(peers))

    def block(dx, z):
        return ((x + dx + NX) % NX) * 2 * NZ + z * 2 + core

    fz = D // FZ

    def spread(z):
        b = block(0, z)
        for d, to in ((0, right_of["x"]), (1, left_of["x"])):
            remote(cot.at[b], cot.at[b], x_s.at[d, z], x_r.at[d, z], to).start()
        remote(cot.at[b], cot.at[b], c_s.at[0, z], c_r.at[0, z], sibling).start()

    def pass_on(z, f, d):
        b = block(0, z)
        piece = cot.at[b, :, pl.ds(f * fz, fz)]
        to = (right_of["z"], left_of["z"])[d]
        return remote(piece, piece, z_s.at[d, z, f], z_r.at[z, f], to)

    for f in range(FZ):
        for d, edge in ((0, zl < NZ - 1), (1, zl > 0)):

            @pl.when(edge)
            def _():
                pass_on(zl, f, d).start()

    spread(zl)

    loads[1].wait()
    for q in range(OWN // QB):
        rows = pl.ds(q * QB, QB)
        weight[node, rows, :] = (
            codes[rows, :].astype(F32) * scales_ref[pl.ds(q, 1), :].astype(F32)
        ).astype(BF16)

    def weight_y(k, n):
        for d, to in ((0, right_of["y"]), (1, left_of["y"])):
            send(weight.at[n], weight.at[n], wy_s.at[k, d], wy_r.at[k, d], to)

    def near(dy):
        return zh * NY + (y + dy + NY) % NY

    def far(dy):
        return (1 - zh) * NY + (y + dy + NY) % NY

    def of(k, dy):
        return (near, far)[k](dy)

    weight_y(0, node)

    for s in range(1, NZ):
        for d in range(2):
            z = zl - s if d == 0 else zl + s
            there = z >= 0 if d == 0 else z < NZ

            @pl.when(there)
            def _():
                for f in range(FZ):
                    piece = cot.at[block(0, z), :, pl.ds(f * fz, fz)]
                    landed(piece, z_r.at[z, f])

                    @pl.when(zl < NZ - 1 if d == 0 else zl > 0)
                    def _():
                        pass_on(z, f, d).start()

                spread(z)

    loads[2].wait()
    hid_t[...] = hid[...].T

    def weight_forward(k):
        for d, to in ((0, right_of["y"]), (1, left_of["y"])):
            n = of(k, -1 if d == 0 else 1)
            landed(weight.at[n], wy_r.at[k, d])
            half = weight.at[n, pl.ds(d * (OWN // 2), OWN // 2), :]
            send(half, half, wh_s.at[k, d], wh_r.at[k, d], to)

    weight_forward(0)

    def slots():
        for s in range(NZ):
            for d in range(2 if s else 1):
                z = zl - s if d == 0 else zl + s
                yield s, z, (z >= 0 if d == 0 else z < NZ)

    for s, z, there in slots():
        @pl.when(there)
        def _():
            for d, to in ((0, right_of["x"]), (1, left_of["x"])):
                b = block(-1 if d == 0 else 1, z)
                landed(cot.at[b], x_r.at[d, z])
                half = cot.at[b, :, pl.ds(d * HALF, HALF)]
                remote(half, half, xh_s.at[d, z], xh_r.at[d, z], to).start()
                remote(cot.at[b], cot.at[b], c_s.at[1 + d, z], c_r.at[1 + d, z], sibling).start()

        if s == 3 :
            pass
    send(weight.at[node], weight.at[node], wz_s.at[0], wz_r.at[0], across)
    for s, z, there in slots():
        @pl.when(there)
        def _():
            for d in range(2):
                half = cot.at[block(2, z), :, pl.ds(d * HALF, HALF)]
                landed(half, xh_r.at[d, z])
                remote(half, half, c_s.at[3 + d, z], c_r.at[3 + d, z], sibling).start()

    def other(dx, z):
        return block(dx, z) + 1 - 2 * core

    for z in range(NZ):
        landed(cot.at[other(0, z)], c_r.at[0, z])
        landed(cot.at[other(-1, z)], c_r.at[1, z])
        landed(cot.at[other(1, z)], c_r.at[2, z])
        for d in range(2):
            landed(cot.at[other(2, z), :, pl.ds(d * HALF, HALF)], c_r.at[3 + d, z])

    def term(n):
        @pl.loop(0, OWN // 256)
        def _(i):
            columns = pl.ds(pl.multiple_of(n * OWN + i * 256, 256), 256)
            rows = cot[:, :, columns].reshape(TOK, 256)
            part[n, :, pl.ds(pl.multiple_of(i * 256, 256), 256)] = jnp.dot(
                hid_t[...], rows, preferred_element_type=F32
            ).astype(BF16)

    hb = FB // 2

    def start_halves(k):
        n = of(k, 2)
        term(n)
        for d, to in ((0, right_of["y"]), (1, left_of["y"])):
            send(
                part.at[n, pl.ds(d * hb, hb), :], yhalf.at[k, d], gh_s.at[k, d], gh_r.at[k, d], to
            )

    def send_neighbours(k):
        for d, to in ((0, right_of["y"]), (1, left_of["y"])):
            n = of(k, 1 if d == 0 else -1)
            landed(yhalf.at[k, d], gh_r.at[k, d])
            rows = pl.ds(d * hb, hb)
            part[n, rows, :] = (
                part[n, rows, :].astype(F32) + yhalf[k, d].astype(F32)
            ).astype(BF16)
            send(part.at[n], ywhole.at[k, d], gy_s.at[k, d], gy_r.at[k, d], to)

    def summed(k):
        for d in range(2):
            landed(ywhole.at[k, d], gy_r.at[k, d])
        return (
            part[of(k, 0)].astype(F32) + ywhole[k, 0].astype(F32) + ywhole[k, 1].astype(F32)
        )

    def hidden_part(k, last):
        @pl.loop(0, TOK // 256)
        def _(i):
            first = pl.multiple_of(i * 256, 256)
            half = (zh if k == 0 else 1 - zh) * HALF
            rows = cot[pl.ds(pl.multiple_of(i * 16, 16), 16), :, pl.ds(pl.multiple_of(half, HALF), HALF)]
            group = (zh if k == 0 else 1 - zh) * NY
            product = jnp.dot(
                rows.reshape(256, HALF),
                weight[pl.ds(group, NY)].reshape(HALF, FB),
                preferred_element_type=F32,
            )
            if last:
                hgrad_ref[pl.ds(first, 256), :] = (hacc[pl.ds(first, 256), :] + product).astype(BF16)
            else:
                hacc[pl.ds(first, 256), :] = product

    def weight_halves(k):
        for d in range(2):
            landed(
                weight.at[of(k, 2), pl.ds(d * (OWN // 2), OWN // 2), :], wh_r.at[k, d]
            )

    start_halves(1)
    term(far(1))
    term(far(-1))
    send_neighbours(1)
    term(far(0))
    start_halves(0)
    term(near(1))
    term(near(-1))
    term(near(0))
    zsum[...] = summed(1).astype(BF16)
    send(zsum, zgot, gz_s.at[0], gz_r.at[0], across)
    send_neighbours(0)
    weight_halves(0)
    hidden_part(0, False)
    near_sum[...] = summed(0)
    landed(weight.at[far(0)], wz_r.at[0])
    weight_y(1, far(0))
    weight_forward(1)
    weight_halves(1)
    hidden_part(1, True)
    landed(zgot, gz_r.at[0])
    total = (near_sum[...] + zgot[...].astype(F32)) * float(TOK * 8) ** -0.5
    wgrad_ref[...] = total.T.astype(BF16)

    for _, copy in sent:
        copy.wait_send()
    for z in range(NZ):
        for d in range(2):
            whole = cot.at[block(0, z)]
            remote(whole, whole, x_s.at[d, z], x_r.at[d, z], sibling).wait_send()
            half = cot.at[block(0, z), :, pl.ds(d * HALF, HALF)]
            remote(half, half, xh_s.at[d, z], xh_r.at[d, z], sibling).wait_send()
            remote(half, half, c_s.at[3 + d, z], c_r.at[3 + d, z], sibling).wait_send()
        for j in range(3):
            remote(whole, whole, c_s.at[j, z], c_r.at[j, z], sibling).wait_send()
        for d in range(2):
            passed = jnp.logical_and(z <= zl, zl < NZ - 1) if d == 0 else jnp.logical_and(z >= zl, zl > 0)

            @pl.when(passed)
            def _():
                for f in range(FZ):
                    pass_on(z, f, d).wait_send()


def body(hidden, cotangent, weight_codes, block_scales):
    dma = pltpu.SemaphoreType.DMA
    hbm = pl.BlockSpec(memory_space=pl.ANY)
    vmem = pl.BlockSpec(memory_space=pltpu.VMEM)
    return pl.pallas_call(
        kernel,
        out_shape=(
            jax.ShapeDtypeStruct((TOK, FB), BF16),
            jax.ShapeDtypeStruct((OWN, FB), BF16),
        ),
        in_specs=[hbm, hbm, hbm, vmem],
        out_specs=(vmem, vmem),
        scratch_shapes=[
            pltpu.VMEM((2 * NX * NZ, ROWS, D), BF16),
            pltpu.VMEM((TOK, FB), BF16),
            pltpu.VMEM((FB, TOK), BF16),
            pltpu.VMEM((OWN, FB), BF16),
            pltpu.VMEM((8, OWN, FB), BF16),
            pltpu.VMEM((8, FB, OWN), BF16),
            pltpu.VMEM((2, 2, FB, OWN), BF16),
            pltpu.VMEM((2, 2, FB // 2, OWN), BF16),
            pltpu.VMEM((FB, OWN), BF16),
            pltpu.VMEM((FB, OWN), BF16),
            pltpu.VMEM((FB, OWN), F32),
            pltpu.VMEM((TOK, FB), F32),
            dma((3,)),
            dma((2, NZ, FZ)), dma((NZ, FZ)),
            dma((2, NZ)), dma((2, NZ)), dma((2, NZ)), dma((2, NZ)),
            dma((5, NZ)), dma((5, NZ)),
            dma((2, 2)), dma((2, 2)), dma((2, 2)), dma((2, 2)),
            dma((1,)), dma((1,)),
            dma((2, 2)), dma((2, 2)), dma((2, 2)), dma((2, 2)),
            dma((1,)), dma((1,)),
        ],
        compiler_params=pltpu.CompilerParams(
            collective_id=0, has_side_effects=True, vmem_limit_bytes=56 << 20
        ),
        cost_estimate=pl.CostEstimate(
            flops=4 * TOK * D * FB, bytes_accessed=4 << 20, transcendentals=0
        ),
    )(hidden, cotangent, weight_codes, block_scales)


def solution(mesh):
    return jax.shard_map(
        body,
        mesh=mesh,
        in_specs=(
            P("node", "wide"),
            P(("node", "wide"), None),
            P("node", "wide"),
            P("node", "wide"),
        ),
        out_specs=(P("node", "wide"), P("node", "wide")),
        check_vma=False,
    )
```

```python
import functools

import jax
import jax.numpy as jnp
from jax import lax
from jax.experimental import pallas as pl
from jax.experimental.pallas import tpu as pltpu
from jax.sharding import PartitionSpec as P

MESH = pl.DeviceIdType.MESH
NX, NY, NZ = 4, 4, 8
D, FB, TOK, ROWS, QB = 4096, 384, 1024, 16, 128
OWN = D // 8
HALF = D // 2
FZ = 2
CW = 4
CG = 3
F32, BF16 = jnp.float32, jnp.bfloat16


def schedule():
    return [('own',), ('weights',), ('turn',), ('z', 1, 0), ('z', 1, 1), ('xf', 0), ('z', 2, 0), ('z', 2, 1), ('z', 3, 0), ('z', 3, 1), ('xf', 1), ('near_weights',), ('z', 4, 0), ('xh', 0), ('z', 4, 1), ('w', 0, 0), ('w', 0, 1), ('w', 0, 2), ('w', 0, 3), ('z', 5, 0), ('z', 5, 1), ('xf', 2), ('near_halves',), ('w', 1, 0), ('w', 1, 1), ('z', 6, 0), ('z', 6, 1), ('w', 1, 2), ('xf', 3), ('w', 1, 3), ('z', 7, 0), ('z', 7, 1), ('xh', 1), ('w', 2, 0), ('w', 2, 1), ('w', 2, 2), ('xf', 4), ('w', 2, 3), ('xh', 2), ('xf', 5), ('w', 3, 0), ('w', 3, 1), ('w', 3, 2), ('xf', 6), ('xh', 3), ('w', 3, 3), ('xf', 7), ('xh', 6), ('w', 4, 0), ('xh', 7), ('xh', 4), ('xh', 5), ('w', 4, 1), ('w', 4, 2), ('w', 4, 3), ('w', 5, 0), ('cores',), ('term', 1, 2), ('w', 5, 1), ('gh', 1, 0), ('gh', 1, 1), ('gh', 1, 2), ('term', 1, 1), ('term', 1, -1), ('w', 5, 2), ('w', 5, 3), ('term', 1, 0), ('term', 0, 2), ('gn', 1, 0), ('gh', 0, 0), ('gh', 0, 1), ('gh', 0, 2), ('term', 0, 1), ('w', 6, 0), ('gn', 1, 1), ('term', 0, -1), ('w', 6, 1), ('term', 0, 0), ('gn', 1, 2), ('hid', 0, 0), ('w', 6, 2), ('hid', 0, 1), ('hid', 0, 2), ('w', 6, 3), ('gs', 0), ('hid', 0, 3), ('w', 7, 0), ('gn', 0, 0), ('w', 7, 1), ('gn', 0, 1), ('w', 7, 2), ('w', 7, 3), ('gn', 0, 2), ('g', 1, 0), ('gs', 1), ('far_weights',), ('gs', 2), ('g', 2, 0), ('g', 1, 1), ('ns', 0), ('g', 1, 2), ('g', 3, 0), ('ns', 1), ('g', 2, 1), ('g', 2, 2), ('ns', 2), ('g', 4, 0), ('g', 3, 1), ('g', 3, 2), ('g', 5, 0), ('g', 4, 1), ('g', 4, 2), ('far_forward',), ('g', 6, 0), ('g', 5, 1), ('g', 5, 2), ('g', 7, 0), ('far_halves',), ('hid', 1, 0), ('hid', 1, 1), ('g', 6, 1), ('hid', 1, 2), ('hid', 1, 3), ('g', 6, 2), ('left', 0), ('end', 0), ('g', 7, 1), ('g', 7, 2), ('end', 1), ('end', 2)]


def kernel(
    hid_hbm, cot_hbm, codes_hbm, scales_ref,
    hgrad_ref, wgrad_ref,
    cot, hid, hid_t, codes, weight, part, ywhole, yhalf, wrelay, grelay, near_sum, hacc,
    local_sem, z_s, z_r, x_s, x_r, xh_s, xh_r, c_s, c_r,
    wy_s, wy_r, wh_s, wh_r, wz_s, wz_r, gy_s, gy_r, gh_s, gh_r, gz_s, gz_r,
):
    wide, node = lax.axis_index("wide"), lax.axis_index("node")
    x, zl, core = wide // (2 * NZ), (wide // 2) % NZ, wide % 2
    zh, y = node // NY, node % NY

    def at(dx=0, dy=0, dz=0):
        z = (zh * NZ + zl + dz + 2 * NZ) % (2 * NZ)
        return (
            ((x + dx + NX) % NX) * 2 * NZ + (z % NZ) * 2 + core,
            (z // NZ) * NY + (y + dy + NY) % NY,
        )

    sibling = (wide + 1 - 2 * core, node)
    ways_x = (at(dx=1), at(dx=-1))
    ways_y = (at(dy=1), at(dy=-1))
    ways_z = (at(dz=1), at(dz=-1))
    def remote(src, dst, s, r, to):
        return pltpu.make_async_remote_copy(
            src_ref=src, dst_ref=dst, send_sem=s, recv_sem=r, device_id=to, device_id_type=MESH
        )

    def send(src, dst, s, r, to):
        remote(src, dst, s, r, to).start()

    def landed(dst, r):
        remote(dst, dst, r, r, sibling).wait_recv()

    def left(src, s):
        remote(src, src, s, s, sibling).wait_send()

    def block(dx, z):
        return ((x + dx + NX) % NX) * 2 * NZ + z * 2 + core

    def near(dy):
        return zh * NY + (y + dy + NY) % NY

    def far(dy):
        return (1 - zh) * NY + (y + dy + NY) % NY

    def of(k, dy):
        return (near, far)[k](dy)


    fz = D // FZ

    def pass_on(z, f, d):
        piece = cot.at[block(0, z), :, pl.ds(f * fz, fz)]
        return remote(piece, piece, z_s.at[d], z_r.at[z, f], ways_z[d])

    def spread(z):
        b = block(0, z)
        for d in range(2):
            remote(cot.at[b], cot.at[b], x_s.at[0], x_r.at[z], ways_x[d]).start()
        remote(cot.at[b], cot.at[b], c_s.at[0], c_r.at[0], sibling).start()

    def go_own():
        for f in range(FZ):
            for d, inside in ((0, zl < NZ - 1), (1, zl > 0)):

                @pl.when(inside)
                def _():
                    pass_on(zl, f, d).start()

        spread(zl)

    def sides(s):
        return [(0, zl - s, zl - s >= 0), (1, zl + s, zl + s < NZ)][: 2 if s else 1]

    def go_z(s, f):
        for d, z, there in sides(s):

            @pl.when(there)
            def _():
                landed(cot.at[block(0, z), :, pl.ds(f * fz, fz)], z_r.at[z, f])

                @pl.when(zl < NZ - 1 if d == 0 else zl > 0)
                def _():
                    pass_on(z, f, d).start()

                if f == FZ - 1:
                    spread(z)

    def half_of(dx, z, d):
        return cot.at[block(dx, z), :, pl.ds(d * HALF, HALF)]

    def go_xf(s):
        for _, z, there in sides(s):

            @pl.when(there)
            def _():
                landed(cot.at[pl.ds(0, 2)], x_r.at[z])
                for d, dx in ((0, -1), (1, 1)):
                    half = half_of(dx, z, d)
                    send(half, half, xh_s.at[0], xh_r.at[z], ways_x[d])
                for dx in (-1, 1):
                    b = block(dx, z)
                    send(cot.at[b], cot.at[b], c_s.at[0], c_r.at[0], sibling)

    def go_xh(s):
        for _, z, there in sides(s):

            @pl.when(there)
            def _():
                b = block(2, z)
                landed(cot.at[b], xh_r.at[z])
                send(cot.at[b], cot.at[b], c_s.at[0], c_r.at[0], sibling)

    def go_cores():
        landed(cot.at[pl.ds(0, NX * NZ)], c_r.at[0])


    def weight_y(k):
        n = of(k, 0)
        for d in range(2):
            send(weight.at[n], weight.at[n], wy_s.at[0], wy_r.at[k, d], ways_y[d])

    def weight_forward(k):
        for d in range(2):
            n = of(k, -1 if d == 0 else 1)
            landed(weight.at[n], wy_r.at[k, d])
            half = weight.at[n, pl.ds(d * (OWN // 2), OWN // 2), :]
            send(half, half, wh_s.at[0], wh_r.at[k], ways_y[d])

    def weight_halves(k):
        landed(weight.at[of(k, 2)], wh_r.at[k])

    def go_weights():
        loads[1].wait()
        for q in range(OWN // QB):
            rows = pl.ds(q * QB, QB)
            weight[node, rows, :] = (
                codes[rows, :].astype(F32) * scales_ref[pl.ds(q, 1), :].astype(F32)
            ).astype(BF16)
        weight_y(0)

    cw = OWN // 2 // CW

    def weight_piece(n, d, c):
        return weight.at[n, pl.ds(d * (OWN // 2) + c * cw, cw), :]

    def go_w(s, c):
        if s:
            landed(wrelay.at[s - 1, c], wz_r.at[s - 1, c])
        for d in range(2):
            src = weight_piece(node, d, c) if s == 0 else wrelay.at[s - 1, c, d]
            dst = wrelay.at[s, c, d]
            if s == NZ - 1:
                z = zh * NZ + zl + (1 if d == 0 else -1) + 2 * NZ
                dst = weight_piece((1 - (z // NZ) % 2) * NY + y, d, c)
            send(src, dst, wz_s.at[0], wz_r.at[s, c], ways_z[d])

    def go_far_weights():
        for c in range(CW):
            landed(wrelay.at[0, c], wz_r.at[NZ - 1, c])
        weight_y(1)


    def go_turn():
        loads[2].wait()
        hid_t[...] = hid[...].T

    def go_term(k, dy):
        n = of(k, dy)

        @pl.loop(0, 2)
        def _(i):
            columns = pl.ds(pl.multiple_of(n * OWN + i * (OWN // 2), OWN // 2), OWN // 2)
            rows = cot[:, :, columns].reshape(TOK, OWN // 2)
            part[n, i] = jnp.dot(hid_t[...], rows, preferred_element_type=F32).astype(BF16)

    cg = FB // CG

    def units(c):
        return pl.ds(c * cg, cg)

    def go_gh(k, c):
        for d in range(2):
            send(
                part.at[of(k, 2), d, units(c), :], yhalf.at[k, d, units(c), :],
                gh_s.at[0], gh_r.at[k, c], ways_y[d],
            )

    def go_gn(k, c):
        landed(yhalf.at[k, :, units(c), :], gh_r.at[k, c])
        for d in range(2):
            n = of(k, 1 if d == 0 else -1)
            part[n, d, units(c), :] = (
                part[n, d, units(c), :].astype(F32) + yhalf[k, d, units(c), :].astype(F32)
            ).astype(BF16)
            send(
                part.at[n, :, units(c), :], ywhole.at[k, d, :, units(c), :],
                gy_s.at[0], gy_r.at[k, c], ways_y[d],
            )

    def summed(k, c):
        landed(ywhole.at[k, :, :, units(c), :], gy_r.at[k, c])
        return (
            part[of(k, 0), :, units(c), :].astype(F32)
            + ywhole[k, 0, :, units(c), :].astype(F32)
            + ywhole[k, 1, :, units(c), :].astype(F32)
        )

    def go_gs(c):
        grelay[0, c] = summed(1, c).astype(BF16)
        go_g(0, c)

    def go_g(s, c):
        if s:
            landed(grelay.at[s, c], gz_r.at[s - 1, c])
        for d in range(2):
            send(
                grelay.at[s, c, d], grelay.at[s + 1, c, d], gz_s.at[0], gz_r.at[s, c], ways_z[d]
            )

    def go_ns(c):
        near_sum[:, units(c), :] = summed(0, c)

    def go_end(c):
        landed(grelay.at[NZ, c], gz_r.at[NZ - 1, c])
        for d in range(2):
            total = near_sum[d, units(c), :] + grelay[NZ, c, d].astype(F32)
            wgrad_ref[pl.ds(d * (OWN // 2), OWN // 2), units(c)] = (
                (total * float(TOK * 8) ** -0.5).T.astype(BF16)
            )


    def go_hid(k, i):
        rows = pl.ds(i * 256, 256)
        group = zh if k == 0 else 1 - zh
        features = pl.ds(pl.multiple_of(group * HALF, HALF), HALF)
        product = jnp.dot(
            cot[pl.ds(i * 16, 16), :, features].reshape(256, HALF),
            weight[pl.ds(group * NY, NY)].reshape(HALF, FB),
            preferred_element_type=F32,
        )
        if k == 0:
            hacc[rows, :] = product
        else:
            hgrad_ref[rows, :] = (hacc[rows, :] + product).astype(BF16)

    def go_left(k):
        if k:
            left(grelay.at[pl.ds(0, NZ)], gz_s.at[0])
            return
        left(cot.at[pl.ds(0, 2 * NZ)], x_s.at[0])
        left(cot.at[pl.ds(0, NZ)], xh_s.at[0])
        left(cot.at[pl.ds(0, NX * NZ)], c_s.at[0])
        for z in range(1, NZ):

            @pl.when(zl == z - 1)
            def _():
                left(cot.at[pl.ds(0, z)], z_s.at[0])

            @pl.when(zl == NZ - z)
            def _():
                left(cot.at[pl.ds(0, z)], z_s.at[1])

        left(weight.at[pl.ds(0, 4)], wy_s.at[0])
        left(weight.at[pl.ds(0, 2)], wh_s.at[0])
        left(weight, wz_s.at[0])
        left(part.at[pl.ds(0, 2)], gh_s.at[0])
        left(part.at[pl.ds(0, 4)], gy_s.at[0])

    barrier = pltpu.get_barrier_semaphore()
    peers = [*ways_x, *ways_y, *ways_z, sibling]
    for peer in peers:
        pl.semaphore_signal(barrier, inc=1, device_id=peer, device_id_type=MESH)
    loads = [
        pltpu.make_async_copy(cot_hbm, cot.at[wide], local_sem.at[0]),
        pltpu.make_async_copy(codes_hbm, codes, local_sem.at[1]),
        pltpu.make_async_copy(hid_hbm, hid, local_sem.at[2]),
    ]
    for load in loads:
        load.start()
    loads[0].wait()
    pl.semaphore_wait(barrier, len(peers))

    steps = {
        "own": go_own, "weights": go_weights, "z": go_z, "xf": go_xf, "xh": go_xh, "cores": go_cores,
        "near_weights": functools.partial(weight_forward, 0), "turn": go_turn, "w": go_w,
        "far_weights": go_far_weights, "far_forward": functools.partial(weight_forward, 1),
        "near_halves": functools.partial(weight_halves, 0),
        "far_halves": functools.partial(weight_halves, 1),
        "term": go_term, "gh": go_gh, "gn": go_gn, "gs": go_gs, "g": go_g, "ns": go_ns,
        "hid": go_hid, "end": go_end, "left": go_left,
    }
    for name, *where in schedule():
        steps[name](*where)

    go_left(1)


def body(hidden, cotangent, weight_codes, block_scales):
    dma = pltpu.SemaphoreType.DMA
    hbm = pl.BlockSpec(memory_space=pl.ANY)
    vmem = pl.BlockSpec(memory_space=pltpu.VMEM)
    return pl.pallas_call(
        kernel,
        out_shape=(
            jax.ShapeDtypeStruct((TOK, FB), BF16),
            jax.ShapeDtypeStruct((OWN, FB), BF16),
        ),
        in_specs=[hbm, hbm, hbm, vmem],
        out_specs=(vmem, vmem),
        scratch_shapes=[
            pltpu.VMEM((2 * NX * NZ, ROWS, D), BF16),
            pltpu.VMEM((TOK, FB), BF16),
            pltpu.VMEM((FB, TOK), BF16),
            pltpu.VMEM((OWN, FB), BF16),
            pltpu.VMEM((8, OWN, FB), BF16),
            pltpu.VMEM((8, 2, FB, OWN // 2), BF16),
            pltpu.VMEM((2, 2, 2, FB, OWN // 2), BF16),
            pltpu.VMEM((2, 2, FB, OWN // 2), BF16),
            pltpu.VMEM((NZ - 1, CW, 2, OWN // 2 // CW, FB), BF16),
            pltpu.VMEM((NZ + 1, CG, 2, FB // CG, OWN // 2), BF16),
            pltpu.VMEM((2, FB, OWN // 2), F32),
            pltpu.VMEM((TOK, FB), F32),
            dma((3,)),
            dma((2,)), dma((NZ, FZ)),
            dma((1,)), dma((NZ,)), dma((1,)), dma((NZ,)),
            dma((1,)), dma((1,)),
            dma((1,)), dma((2, 2)), dma((1,)), dma((2,)),
            dma((1,)), dma((NZ, CW)),
            dma((1,)), dma((2, CG)), dma((1,)), dma((2, CG)),
            dma((1,)), dma((NZ, CG)),
        ],
        compiler_params=pltpu.CompilerParams(
            collective_id=0, has_side_effects=True, vmem_limit_bytes=56 << 20
        ),
        cost_estimate=pl.CostEstimate(
            flops=4 * TOK * D * FB, bytes_accessed=4 << 20, transcendentals=0
        ),
    )(hidden, cotangent, weight_codes, block_scales)


def solution(mesh):
    return jax.shard_map(
        body,
        mesh=mesh,
        in_specs=(
            P("node", "wide"),
            P(("node", "wide"), None),
            P("node", "wide"),
            P("node", "wide"),
        ),
        out_specs=(P("node", "wide"), P("node", "wide")),
        check_vma=False,
    )
```

```python
import functools

import jax
import jax.numpy as jnp
from jax import lax
from jax.experimental import pallas as pl
from jax.experimental.pallas import tpu as pltpu
from jax.sharding import PartitionSpec as P

MESH = pl.DeviceIdType.MESH
NX, NY, NZ = 4, 4, 8
D, FB, TOK, ROWS, QB = 4096, 384, 1024, 16, 128
OWN = D // 8
HALF = D // 2
FZ = 4
CW = 4
CG = 3
WH = 1
GH = 1
WS, GS = NZ // WH, NZ // GH
F32, BF16 = jnp.float32, jnp.bfloat16


def schedule():
    return [
        ("own",), ("weights",), ("w", 0, 0), ("z", 1, 0), ("z", 1, 1), ("z", 1, 2), ("z", 1, 3),
        ("xf", 0), ("w", 0, 1), ("z", 2, 0), ("z", 2, 1), ("z", 2, 2), ("z", 2, 3), ("z", 3, 0),
        ("z", 3, 1), ("z", 3, 2), ("z", 3, 3), ("w", 0, 2), ("z", 4, 0), ("z", 4, 1), ("xf", 1),
        ("near_weights",), ("z", 4, 2), ("z", 4, 3), ("w", 0, 3), ("z", 5, 0), ("z", 5, 1),
        ("z", 5, 2), ("z", 5, 3), ("xf", 2), ("w", 1, 0), ("z", 6, 0), ("z", 6, 1), ("z", 6, 2),
        ("z", 6, 3), ("w", 1, 1), ("z", 7, 0), ("w", 1, 2), ("xf", 3), ("z", 7, 1), ("z", 7, 2),
        ("w", 1, 3), ("z", 7, 3), ("w", 2, 0), ("xh", 1), ("w", 2, 1), ("w", 2, 2), ("xf", 4),
        ("w", 2, 3), ("xf", 5), ("w", 3, 0), ("turn",), ("xf", 6), ("w", 3, 1), ("xh", 0),
        ("xf", 7), ("w", 3, 2), ("xh", 2), ("w", 3, 3), ("xh", 3), ("w", 4, 0), ("xh", 5),
        ("w", 4, 1), ("xh", 4), ("xh", 6), ("w", 4, 2), ("xh", 7), ("w", 4, 3), ("near_halves",),
        ("cores",), ("w", 5, 0), ("term", 1, 2), ("gh", 1, 0), ("w", 5, 1), ("gh", 1, 2),
        ("gh", 1, 1), ("w", 5, 2), ("term", 0, 2), ("w", 5, 3), ("term", 1, 1), ("w", 6, 0),
        ("term", 1, -1), ("gn", 1, 0), ("w", 6, 1), ("term", 0, 1), ("gn", 1, 2), ("w", 6, 2),
        ("gn", 1, 1), ("w", 6, 3), ("w", 7, 0), ("w", 7, 1), ("hid", 0, 3), ("w", 7, 2),
        ("term", 1, 0), ("gs", 0), ("gh", 0, 0), ("gh", 0, 1), ("term", 0, -1), ("w", 7, 3),
        ("gs", 2), ("gs", 1), ("gh", 0, 2), ("hid", 0, 0), ("far_weights",), ("g", 1, 0),
        ("g", 1, 2), ("g", 1, 1), ("g", 2, 0), ("gn", 0, 2), ("g", 2, 2), ("g", 2, 1),
        ("term", 0, 0), ("g", 3, 0), ("g", 3, 2), ("g", 3, 1), ("far_forward",), ("hid", 0, 1),
        ("g", 4, 0), ("g", 4, 2), ("g", 4, 1), ("g", 5, 0), ("ns", 2), ("g", 5, 2), ("far_halves",),
        ("gn", 0, 1), ("g", 5, 1), ("g", 6, 0), ("g", 6, 2), ("hid", 0, 2), ("gn", 0, 0),
        ("g", 6, 1), ("ns", 1), ("g", 7, 0), ("hid", 1, 3), ("g", 7, 2), ("hid", 1, 2), ("g", 7, 1),
        ("ns", 0), ("left", 0), ("end", 0), ("hid", 1, 0), ("end", 2), ("hid", 1, 1), ("end", 1),
    ]


def kernel(
    hid_hbm, cot_hbm, codes_hbm, scales_ref,
    hgrad_ref, wgrad_ref,
    cot, hid, hid_t, codes, weight, part, ywhole, yhalf, wrelay, grelay, near_sum, hacc,
    local_sem, z_s, z_r, x_s, x_r, xh_s, xh_r, c_s, c_r,
    wy_s, wy_r, wh_s, wh_r, wz_s, wz_r, gy_s, gy_r, gh_s, gh_r, gz_s, gz_r,
):
    wide, node = lax.axis_index("wide"), lax.axis_index("node")
    x, zl, core = wide // (2 * NZ), (wide // 2) % NZ, wide % 2
    zh, y = node // NY, node % NY

    def at(dx=0, dy=0, dz=0):
        z = (zh * NZ + zl + dz + 2 * NZ) % (2 * NZ)
        return (
            ((x + dx + NX) % NX) * 2 * NZ + (z % NZ) * 2 + core,
            (z // NZ) * NY + (y + dy + NY) % NY,
        )

    sibling = (wide + 1 - 2 * core, node)
    ways_x = (at(dx=1), at(dx=-1))
    ways_y = (at(dy=1), at(dy=-1))
    ways_z = (at(dz=1), at(dz=-1))
    ways_w = (at(dz=WH), at(dz=-WH))
    ways_g = (at(dz=GH), at(dz=-GH))
    def remote(src, dst, s, r, to):
        return pltpu.make_async_remote_copy(
            src_ref=src, dst_ref=dst, send_sem=s, recv_sem=r, device_id=to, device_id_type=MESH
        )

    def send(src, dst, s, r, to):
        remote(src, dst, s, r, to).start()

    def landed(dst, r):
        remote(dst, dst, r, r, sibling).wait_recv()

    def left(src, s):
        remote(src, src, s, s, sibling).wait_send()

    def block(dx, z):
        return ((x + dx + NX) % NX) * 2 * NZ + z * 2 + core

    def near(dy):
        return zh * NY + (y + dy + NY) % NY

    def far(dy):
        return (1 - zh) * NY + (y + dy + NY) % NY

    def of(k, dy):
        return (near, far)[k](dy)


    fz = D // FZ

    def pass_on(z, f, d):
        piece = cot.at[block(0, z), :, pl.ds(f * fz, fz)]
        return remote(piece, piece, z_s.at[d], z_r.at[z, f], ways_z[d])

    def spread(z):
        b = block(0, z)
        for d in range(2):
            remote(cot.at[b], cot.at[b], x_s.at[0], x_r.at[z], ways_x[d]).start()
        remote(cot.at[b], cot.at[b], c_s.at[0], c_r.at[0], sibling).start()

    def go_own():
        for f in range(FZ):
            for d, inside in ((0, zl < NZ - 1), (1, zl > 0)):

                @pl.when(inside)
                def _():
                    pass_on(zl, f, d).start()

        spread(zl)

    def sides(s):
        return [(0, zl - s, zl - s >= 0), (1, zl + s, zl + s < NZ)][: 2 if s else 1]

    def go_z(s, f):
        for d, z, there in sides(s):

            @pl.when(there)
            def _():
                landed(cot.at[block(0, z), :, pl.ds(f * fz, fz)], z_r.at[z, f])

                @pl.when(zl < NZ - 1 if d == 0 else zl > 0)
                def _():
                    pass_on(z, f, d).start()

                if f == FZ - 1:
                    spread(z)

    def half_of(dx, z, d):
        return cot.at[block(dx, z), :, pl.ds(d * HALF, HALF)]

    def go_xf(s):
        for _, z, there in sides(s):

            @pl.when(there)
            def _():
                landed(cot.at[pl.ds(0, 2)], x_r.at[z])
                for d, dx in ((0, -1), (1, 1)):
                    half = half_of(dx, z, d)
                    send(half, half, xh_s.at[0], xh_r.at[z], ways_x[d])
                for dx in (-1, 1):
                    b = block(dx, z)
                    send(cot.at[b], cot.at[b], c_s.at[0], c_r.at[0], sibling)

    def go_xh(s):
        for _, z, there in sides(s):

            @pl.when(there)
            def _():
                b = block(2, z)
                landed(cot.at[b], xh_r.at[z])
                send(cot.at[b], cot.at[b], c_s.at[0], c_r.at[0], sibling)

    def go_cores():
        landed(cot.at[pl.ds(0, NX * NZ)], c_r.at[0])


    def weight_y(k):
        n = of(k, 0)
        for d in range(2):
            send(weight.at[n], weight.at[n], wy_s.at[0], wy_r.at[k, d], ways_y[d])

    def weight_forward(k):
        for d in range(2):
            n = of(k, -1 if d == 0 else 1)
            landed(weight.at[n], wy_r.at[k, d])
            half = weight.at[n, pl.ds(d * (OWN // 2), OWN // 2), :]
            send(half, half, wh_s.at[0], wh_r.at[k], ways_y[d])

    def weight_halves(k):
        landed(weight.at[of(k, 2)], wh_r.at[k])

    def go_weights():
        loads[1].wait()
        for q in range(OWN // QB):
            rows = pl.ds(q * QB, QB)
            weight[node, rows, :] = (
                codes[rows, :].astype(F32) * scales_ref[pl.ds(q, 1), :].astype(F32)
            ).astype(BF16)
        weight_y(0)

    cw = OWN // 2 // CW

    def weight_piece(n, d, c):
        return weight.at[n, pl.ds(d * (OWN // 2) + c * cw, cw), :]

    def go_w(s, c):
        if s:
            landed(wrelay.at[s - 1, c], wz_r.at[s - 1, c])
        for d in range(2):
            src = weight_piece(node, d, c) if s == 0 else wrelay.at[s - 1, c, d]
            dst = wrelay.at[min(s, WS - 2), c, d]
            if s == WS - 1:
                z = zh * NZ + zl + (WH if d == 0 else -WH) + 2 * NZ
                dst = weight_piece((1 - (z // NZ) % 2) * NY + y, d, c)
            send(src, dst, wz_s.at[0], wz_r.at[s, c], ways_w[d])

    def go_far_weights():
        for c in range(CW):
            landed(wrelay.at[0, c], wz_r.at[WS - 1, c])
        weight_y(1)


    def go_turn():
        loads[2].wait()
        hid_t[...] = hid[...].T

    def go_term(k, dy):
        n = of(k, dy)

        @pl.loop(0, 2)
        def _(i):
            columns = pl.ds(pl.multiple_of(n * OWN + i * (OWN // 2), OWN // 2), OWN // 2)
            rows = cot[:, :, columns].reshape(TOK, OWN // 2)
            part[n, i] = jnp.dot(hid_t[...], rows, preferred_element_type=F32).astype(BF16)

    cg = FB // CG

    def units(c):
        return pl.ds(c * cg, cg)

    def go_gh(k, c):
        for d in range(2):
            send(
                part.at[of(k, 2), d, units(c), :], yhalf.at[k, d, units(c), :],
                gh_s.at[0], gh_r.at[k, c], ways_y[d],
            )

    def go_gn(k, c):
        landed(yhalf.at[k, :, units(c), :], gh_r.at[k, c])
        for d in range(2):
            n = of(k, 1 if d == 0 else -1)
            part[n, d, units(c), :] = (
                part[n, d, units(c), :].astype(F32) + yhalf[k, d, units(c), :].astype(F32)
            ).astype(BF16)
            send(
                part.at[n, :, units(c), :], ywhole.at[k, d, :, units(c), :],
                gy_s.at[0], gy_r.at[k, c], ways_y[d],
            )

    def summed(k, c):
        landed(ywhole.at[k, :, :, units(c), :], gy_r.at[k, c])
        return (
            part[of(k, 0), :, units(c), :].astype(F32)
            + ywhole[k, 0, :, units(c), :].astype(F32)
            + ywhole[k, 1, :, units(c), :].astype(F32)
        )

    def go_gs(c):
        grelay[0, c] = summed(1, c).astype(BF16)
        go_g(0, c)

    def go_g(s, c):
        if s:
            landed(grelay.at[s, c], gz_r.at[s - 1, c])
        for d in range(2):
            send(
                grelay.at[s, c, d], grelay.at[s + 1, c, d], gz_s.at[0], gz_r.at[s, c], ways_g[d]
            )

    def go_ns(c):
        near_sum[:, units(c), :] = summed(0, c)

    def go_end(c):
        landed(grelay.at[GS, c], gz_r.at[GS - 1, c])
        for d in range(2):
            total = near_sum[d, units(c), :] + grelay[GS, c, d].astype(F32)
            wgrad_ref[pl.ds(d * (OWN // 2), OWN // 2), units(c)] = (
                (total * float(TOK * 8) ** -0.5).T.astype(BF16)
            )


    def go_hid(k, i):
        rows = pl.ds(i * 256, 256)
        group = zh if k == 0 else 1 - zh
        features = pl.ds(pl.multiple_of(group * HALF, HALF), HALF)
        product = jnp.dot(
            cot[pl.ds(i * 16, 16), :, features].reshape(256, HALF),
            weight[pl.ds(group * NY, NY)].reshape(HALF, FB),
            preferred_element_type=F32,
        )
        if k == 0:
            hacc[rows, :] = product
        else:
            hgrad_ref[rows, :] = (hacc[rows, :] + product).astype(BF16)

    def go_left(k):
        if k:
            left(grelay.at[pl.ds(0, GS)], gz_s.at[0])
            return
        left(cot.at[pl.ds(0, 2 * NZ)], x_s.at[0])
        left(cot.at[pl.ds(0, NZ)], xh_s.at[0])
        left(cot.at[pl.ds(0, NX * NZ)], c_s.at[0])
        for z in range(1, NZ):

            @pl.when(zl == z - 1)
            def _():
                left(cot.at[pl.ds(0, z)], z_s.at[0])

            @pl.when(zl == NZ - z)
            def _():
                left(cot.at[pl.ds(0, z)], z_s.at[1])

        left(weight.at[pl.ds(0, 4)], wy_s.at[0])
        left(weight.at[pl.ds(0, 2)], wh_s.at[0])
        left(weight.at[pl.ds(0, WS)], wz_s.at[0])
        left(part.at[pl.ds(0, 2)], gh_s.at[0])
        left(part.at[pl.ds(0, 4)], gy_s.at[0])

    barrier = pltpu.get_barrier_semaphore()
    peers = [*ways_x, *ways_y, *ways_z, sibling]
    for hop in sorted({WH, GH} - {1}):
        peers += (at(dz=hop), at(dz=-hop))
    for peer in peers:
        pl.semaphore_signal(barrier, inc=1, device_id=peer, device_id_type=MESH)
    loads = [
        pltpu.make_async_copy(cot_hbm, cot.at[wide], local_sem.at[0]),
        pltpu.make_async_copy(codes_hbm, codes, local_sem.at[1]),
        pltpu.make_async_copy(hid_hbm, hid, local_sem.at[2]),
    ]
    for load in loads:
        load.start()
    loads[0].wait()
    pl.semaphore_wait(barrier, len(peers))

    steps = {
        "own": go_own, "weights": go_weights, "z": go_z, "xf": go_xf, "xh": go_xh, "cores": go_cores,
        "near_weights": functools.partial(weight_forward, 0), "turn": go_turn, "w": go_w,
        "far_weights": go_far_weights, "far_forward": functools.partial(weight_forward, 1),
        "near_halves": functools.partial(weight_halves, 0),
        "far_halves": functools.partial(weight_halves, 1),
        "term": go_term, "gh": go_gh, "gn": go_gn, "gs": go_gs, "g": go_g, "ns": go_ns,
        "hid": go_hid, "end": go_end, "left": go_left,
    }
    for name, *where in schedule():
        steps[name](*where)

    go_left(1)


def body(hidden, cotangent, weight_codes, block_scales):
    dma = pltpu.SemaphoreType.DMA
    hbm = pl.BlockSpec(memory_space=pl.ANY)
    vmem = pl.BlockSpec(memory_space=pltpu.VMEM)
    return pl.pallas_call(
        kernel,
        out_shape=(
            jax.ShapeDtypeStruct((TOK, FB), BF16),
            jax.ShapeDtypeStruct((OWN, FB), BF16),
        ),
        in_specs=[hbm, hbm, hbm, vmem],
        out_specs=(vmem, vmem),
        scratch_shapes=[
            pltpu.VMEM((2 * NX * NZ, ROWS, D), BF16),
            pltpu.VMEM((TOK, FB), BF16),
            pltpu.VMEM((FB, TOK), BF16),
            pltpu.VMEM((OWN, FB), BF16),
            pltpu.VMEM((8, OWN, FB), BF16),
            pltpu.VMEM((8, 2, FB, OWN // 2), BF16),
            pltpu.VMEM((2, 2, 2, FB, OWN // 2), BF16),
            pltpu.VMEM((2, 2, FB, OWN // 2), BF16),
            pltpu.VMEM((WS - 1, CW, 2, OWN // 2 // CW, FB), BF16),
            pltpu.VMEM((GS + 1, CG, 2, FB // CG, OWN // 2), BF16),
            pltpu.VMEM((2, FB, OWN // 2), F32),
            pltpu.VMEM((TOK, FB), F32),
            dma((3,)),
            dma((2,)), dma((NZ, FZ)),
            dma((1,)), dma((NZ,)), dma((1,)), dma((NZ,)),
            dma((1,)), dma((1,)),
            dma((1,)), dma((2, 2)), dma((1,)), dma((2,)),
            dma((1,)), dma((WS, CW)),
            dma((1,)), dma((2, CG)), dma((1,)), dma((2, CG)),
            dma((1,)), dma((GS, CG)),
        ],
        compiler_params=pltpu.CompilerParams(
            collective_id=0, has_side_effects=True, vmem_limit_bytes=56 << 20
        ),
        cost_estimate=pl.CostEstimate(
            flops=4 * TOK * D * FB, bytes_accessed=4 << 20, transcendentals=0
        ),
    )(hidden, cotangent, weight_codes, block_scales)


def solution(mesh):
    return jax.shard_map(
        body,
        mesh=mesh,
        in_specs=(
            P("node", "wide"),
            P(("node", "wide"), None),
            P("node", "wide"),
            P("node", "wide"),
        ),
        out_specs=(P("node", "wide"), P("node", "wide")),
        check_vma=False,
    )
```

```python
import functools

import jax
import jax.numpy as jnp
from jax import lax
from jax.experimental import pallas as pl
from jax.experimental.pallas import tpu as pltpu
from jax.sharding import PartitionSpec as P

MESH = pl.DeviceIdType.MESH
NX, NY, NZ = 4, 4, 8
D, FB, TOK, ROWS, QB = 4096, 384, 1024, 16, 128
OWN = D // 8
HALF = D // 2
FZ = 4
CW = 4
CG = 3
WH = 1
GH = 1
WS, GS = NZ // WH, NZ // GH
F32, BF16 = jnp.float32, jnp.bfloat16


def schedule():
    return [
        ("own",), ("weights",), ("w", 0, 0), ("z", 1, 0), ("z", 1, 1), ("z", 1, 2), ("z", 1, 3),
        ("xf", 0), ("w", 0, 1), ("z", 2, 0), ("z", 2, 1), ("z", 2, 2), ("z", 2, 3), ("z", 3, 0),
        ("z", 3, 1), ("z", 3, 2), ("z", 3, 3), ("w", 0, 2), ("z", 4, 0), ("z", 4, 1), ("xf", 1),
        ("near_weights",), ("z", 4, 2), ("z", 4, 3), ("w", 0, 3), ("z", 5, 0), ("z", 5, 1),
        ("z", 5, 2), ("z", 5, 3), ("xf", 2), ("w", 1, 0), ("z", 6, 0), ("z", 6, 1), ("z", 6, 2),
        ("z", 6, 3), ("w", 1, 1), ("z", 7, 0), ("w", 1, 2), ("xf", 3), ("z", 7, 1), ("z", 7, 2),
        ("w", 1, 3), ("z", 7, 3), ("w", 2, 0), ("xh", 1), ("w", 2, 1), ("w", 2, 2), ("xf", 4),
        ("w", 2, 3), ("xf", 5), ("w", 3, 0), ("turn",), ("xf", 6), ("w", 3, 1), ("xh", 0),
        ("xf", 7), ("w", 3, 2), ("xh", 2), ("w", 3, 3), ("xh", 3), ("w", 4, 0), ("xh", 5),
        ("w", 4, 1), ("xh", 4), ("xh", 6), ("w", 4, 2), ("xh", 7), ("w", 4, 3), ("near_halves",),
        ("cores",), ("w", 5, 0), ("term", 1, 2), ("gh", 1, 0), ("w", 5, 1), ("gh", 1, 2),
        ("gh", 1, 1), ("w", 5, 2), ("term", 0, 2), ("w", 5, 3), ("term", 1, 1), ("w", 6, 0),
        ("term", 1, -1), ("gn", 1, 0), ("w", 6, 1), ("term", 0, 1), ("gn", 1, 2), ("w", 6, 2),
        ("gn", 1, 1), ("w", 6, 3), ("w", 7, 0), ("w", 7, 1), ("hid", 0, 3), ("w", 7, 2),
        ("term", 1, 0), ("gs", 0), ("gh", 0, 0), ("gh", 0, 1), ("term", 0, -1), ("w", 7, 3),
        ("gs", 2), ("gs", 1), ("gh", 0, 2), ("hid", 0, 0), ("far_weights",), ("g", 1, 0),
        ("g", 1, 2), ("g", 1, 1), ("g", 2, 0), ("gn", 0, 2), ("g", 2, 2), ("g", 2, 1),
        ("term", 0, 0), ("g", 3, 0), ("g", 3, 2), ("g", 3, 1), ("far_forward",), ("hid", 0, 1),
        ("g", 4, 0), ("g", 4, 2), ("g", 4, 1), ("g", 5, 0), ("ns", 2), ("g", 5, 2), ("far_halves",),
        ("gn", 0, 1), ("g", 5, 1), ("g", 6, 0), ("g", 6, 2), ("hid", 0, 2), ("gn", 0, 0),
        ("g", 6, 1), ("ns", 1), ("g", 7, 0), ("hid", 1, 3), ("g", 7, 2), ("hid", 1, 2), ("g", 7, 1),
        ("ns", 0), ("left", 0), ("end", 0), ("hid", 1, 0), ("end", 2), ("hid", 1, 1), ("end", 1),
    ]


def kernel(
    hid_hbm, cot_hbm, codes_hbm, scales_hbm,
    hgrad_ref, wgrad_ref,
    cot, hid, hid_t, codes, scales, weight, part, ywhole, yhalf, wrelay, grelay, near_sum, hacc,
    local_sem, z_s, z_r, x_s, x_r, xh_s, xh_r, c_s, c_r,
    wy_s, wy_r, wh_s, wh_r, wz_s, wz_r, gy_s, gy_r, gh_s, gh_r, gz_s, gz_r,
):
    wide, node = lax.axis_index("wide"), lax.axis_index("node")
    x, zl, core = wide // (2 * NZ), (wide // 2) % NZ, wide % 2
    zh, y = node // NY, node % NY

    def at(dx=0, dy=0, dz=0):
        z = (zh * NZ + zl + dz + 2 * NZ) % (2 * NZ)
        return (
            ((x + dx + NX) % NX) * 2 * NZ + (z % NZ) * 2 + core,
            (z // NZ) * NY + (y + dy + NY) % NY,
        )

    sibling = (wide + 1 - 2 * core, node)
    ways_x = (at(dx=1), at(dx=-1))
    ways_y = (at(dy=1), at(dy=-1))
    ways_z = (at(dz=1), at(dz=-1))
    ways_w = (at(dz=WH), at(dz=-WH))
    ways_g = (at(dz=GH), at(dz=-GH))
    def remote(src, dst, s, r, to):
        return pltpu.make_async_remote_copy(
            src_ref=src, dst_ref=dst, send_sem=s, recv_sem=r, device_id=to, device_id_type=MESH
        )

    def send(src, dst, s, r, to):
        remote(src, dst, s, r, to).start()

    def landed(dst, r):
        remote(dst, dst, r, r, sibling).wait_recv()

    def left(src, s):
        remote(src, src, s, s, sibling).wait_send()

    def block(dx, z):
        return ((x + dx + NX) % NX) * 2 * NZ + z * 2 + core

    def near(dy):
        return zh * NY + (y + dy + NY) % NY

    def far(dy):
        return (1 - zh) * NY + (y + dy + NY) % NY

    def of(k, dy):
        return (near, far)[k](dy)


    fz = D // FZ

    def pass_on(z, f, d):
        piece = cot.at[block(0, z), :, pl.ds(f * fz, fz)]
        return remote(piece, piece, z_s.at[d], z_r.at[z, f], ways_z[d])

    def spread(z):
        b = block(0, z)
        for d in range(2):
            remote(cot.at[b], cot.at[b], x_s.at[0], x_r.at[z], ways_x[d]).start()
        remote(cot.at[b], cot.at[b], c_s.at[0], c_r.at[0], sibling).start()

    def go_own():
        for f in range(FZ):
            for d, inside in ((0, zl < NZ - 1), (1, zl > 0)):

                @pl.when(inside)
                def _():
                    pass_on(zl, f, d).start()

        spread(zl)

    def sides(s):
        return [(0, zl - s, zl - s >= 0), (1, zl + s, zl + s < NZ)][: 2 if s else 1]

    def go_z(s, f):
        for d, z, there in sides(s):

            @pl.when(there)
            def _():
                landed(cot.at[block(0, z), :, pl.ds(f * fz, fz)], z_r.at[z, f])

                @pl.when(zl < NZ - 1 if d == 0 else zl > 0)
                def _():
                    pass_on(z, f, d).start()

                if f == FZ - 1:
                    spread(z)

    def half_of(dx, z, d):
        return cot.at[block(dx, z), :, pl.ds(d * HALF, HALF)]

    def go_xf(s):
        for _, z, there in sides(s):

            @pl.when(there)
            def _():
                landed(cot.at[pl.ds(0, 2)], x_r.at[z])
                for d, dx in ((0, -1), (1, 1)):
                    half = half_of(dx, z, d)
                    send(half, half, xh_s.at[0], xh_r.at[z], ways_x[d])
                for dx in (-1, 1):
                    b = block(dx, z)
                    send(cot.at[b], cot.at[b], c_s.at[0], c_r.at[0], sibling)

    def go_xh(s):
        for _, z, there in sides(s):

            @pl.when(there)
            def _():
                b = block(2, z)
                landed(cot.at[b], xh_r.at[z])
                send(cot.at[b], cot.at[b], c_s.at[0], c_r.at[0], sibling)

    def go_cores():
        landed(cot.at[pl.ds(0, NX * NZ)], c_r.at[0])


    def weight_y(k):
        n = of(k, 0)
        for d in range(2):
            send(weight.at[n], weight.at[n], wy_s.at[0], wy_r.at[k, d], ways_y[d])

    def weight_forward(k):
        for d in range(2):
            n = of(k, -1 if d == 0 else 1)
            landed(weight.at[n], wy_r.at[k, d])
            half = weight.at[n, pl.ds(d * (OWN // 2), OWN // 2), :]
            send(half, half, wh_s.at[0], wh_r.at[k], ways_y[d])

    def weight_halves(k):
        landed(weight.at[of(k, 2)], wh_r.at[k])

    def go_weights():
        loads[1].wait()
        loads[3].wait()
        for q in range(OWN // QB):
            rows = pl.ds(q * QB, QB)
            weight[node, rows, :] = (
                codes[rows, :].astype(F32) * scales[pl.ds(q, 1), :].astype(F32)
            ).astype(BF16)
        weight_y(0)

    cw = OWN // 2 // CW

    def weight_piece(n, d, c):
        return weight.at[n, pl.ds(d * (OWN // 2) + c * cw, cw), :]

    def go_w(s, c):
        if s:
            landed(wrelay.at[s - 1, c], wz_r.at[s - 1, c])
        for d in range(2):
            src = weight_piece(node, d, c) if s == 0 else wrelay.at[s - 1, c, d]
            dst = wrelay.at[min(s, WS - 2), c, d]
            if s == WS - 1:
                z = zh * NZ + zl + (WH if d == 0 else -WH) + 2 * NZ
                dst = weight_piece((1 - (z // NZ) % 2) * NY + y, d, c)
            send(src, dst, wz_s.at[0], wz_r.at[s, c], ways_w[d])

    def go_far_weights():
        for c in range(CW):
            landed(wrelay.at[0, c], wz_r.at[WS - 1, c])
        weight_y(1)


    def go_turn():
        loads[2].wait()
        hid_t[...] = hid[...].T

    def go_term(k, dy):
        n = of(k, dy)

        @pl.loop(0, 2)
        def _(i):
            columns = pl.ds(pl.multiple_of(n * OWN + i * (OWN // 2), OWN // 2), OWN // 2)
            rows = cot[:, :, columns].reshape(TOK, OWN // 2)
            part[n, i] = jnp.dot(hid_t[...], rows, preferred_element_type=F32).astype(BF16)

    cg = FB // CG

    def units(c):
        return pl.ds(c * cg, cg)

    def go_gh(k, c):
        for d in range(2):
            send(
                part.at[of(k, 2), d, units(c), :], yhalf.at[k, d, units(c), :],
                gh_s.at[0], gh_r.at[k, c], ways_y[d],
            )

    def go_gn(k, c):
        landed(yhalf.at[k, :, units(c), :], gh_r.at[k, c])
        for d in range(2):
            n = of(k, 1 if d == 0 else -1)
            part[n, d, units(c), :] = (
                part[n, d, units(c), :].astype(F32) + yhalf[k, d, units(c), :].astype(F32)
            ).astype(BF16)
            send(
                part.at[n, :, units(c), :], ywhole.at[k, d, :, units(c), :],
                gy_s.at[0], gy_r.at[k, c], ways_y[d],
            )

    def summed(k, c):
        landed(ywhole.at[k, :, :, units(c), :], gy_r.at[k, c])
        return (
            part[of(k, 0), :, units(c), :].astype(F32)
            + ywhole[k, 0, :, units(c), :].astype(F32)
            + ywhole[k, 1, :, units(c), :].astype(F32)
        )

    def go_gs(c):
        grelay[0, c] = summed(1, c).astype(BF16)
        go_g(0, c)

    def go_g(s, c):
        if s:
            landed(grelay.at[s, c], gz_r.at[s - 1, c])
        for d in range(2):
            send(
                grelay.at[s, c, d], grelay.at[s + 1, c, d], gz_s.at[0], gz_r.at[s, c], ways_g[d]
            )

    def go_ns(c):
        near_sum[:, units(c), :] = summed(0, c)

    def go_end(c):
        landed(grelay.at[GS, c], gz_r.at[GS - 1, c])
        for d in range(2):
            total = near_sum[d, units(c), :] + grelay[GS, c, d].astype(F32)
            wgrad_ref[pl.ds(d * (OWN // 2), OWN // 2), units(c)] = (
                (total * float(TOK * 8) ** -0.5).T.astype(BF16)
            )


    def go_hid(k, i):
        rows = pl.ds(i * 256, 256)
        group = zh if k == 0 else 1 - zh
        features = pl.ds(pl.multiple_of(group * HALF, HALF), HALF)
        product = jnp.dot(
            cot[pl.ds(i * 16, 16), :, features].reshape(256, HALF),
            weight[pl.ds(group * NY, NY)].reshape(HALF, FB),
            preferred_element_type=F32,
        )
        if k == 0:
            hacc[rows, :] = product
        else:
            hgrad_ref[rows, :] = (hacc[rows, :] + product).astype(BF16)

    def go_left(k):
        if k:
            left(grelay.at[pl.ds(0, GS)], gz_s.at[0])
            return
        left(cot.at[pl.ds(0, 2 * NZ)], x_s.at[0])
        left(cot.at[pl.ds(0, NZ)], xh_s.at[0])
        left(cot.at[pl.ds(0, NX * NZ)], c_s.at[0])
        for z in range(1, NZ):

            @pl.when(zl == z - 1)
            def _():
                left(cot.at[pl.ds(0, z)], z_s.at[0])

            @pl.when(zl == NZ - z)
            def _():
                left(cot.at[pl.ds(0, z)], z_s.at[1])

        left(weight.at[pl.ds(0, 4)], wy_s.at[0])
        left(weight.at[pl.ds(0, 2)], wh_s.at[0])
        left(weight.at[pl.ds(0, WS)], wz_s.at[0])
        left(part.at[pl.ds(0, 2)], gh_s.at[0])
        left(part.at[pl.ds(0, 4)], gy_s.at[0])

    barrier = pltpu.get_barrier_semaphore()
    peers = [*ways_x, *ways_y, *ways_z, sibling]
    for hop in sorted({WH, GH} - {1}):
        peers += (at(dz=hop), at(dz=-hop))
    for peer in peers:
        pl.semaphore_signal(barrier, inc=1, device_id=peer, device_id_type=MESH)
    loads = [
        pltpu.make_async_copy(cot_hbm, cot.at[wide], local_sem.at[0]),
        pltpu.make_async_copy(codes_hbm, codes, local_sem.at[1]),
        pltpu.make_async_copy(hid_hbm, hid, local_sem.at[2]),
        pltpu.make_async_copy(scales_hbm, scales, local_sem.at[3]),
    ]
    for load in loads:
        load.start()
    loads[0].wait()
    pl.semaphore_wait(barrier, len(peers))

    steps = {
        "own": go_own, "weights": go_weights, "z": go_z, "xf": go_xf, "xh": go_xh, "cores": go_cores,
        "near_weights": functools.partial(weight_forward, 0), "turn": go_turn, "w": go_w,
        "far_weights": go_far_weights, "far_forward": functools.partial(weight_forward, 1),
        "near_halves": functools.partial(weight_halves, 0),
        "far_halves": functools.partial(weight_halves, 1),
        "term": go_term, "gh": go_gh, "gn": go_gn, "gs": go_gs, "g": go_g, "ns": go_ns,
        "hid": go_hid, "end": go_end, "left": go_left,
    }
    for name, *where in schedule():
        steps[name](*where)

    go_left(1)


def body(hidden, cotangent, weight_codes, block_scales):
    dma = pltpu.SemaphoreType.DMA
    hbm = pl.BlockSpec(memory_space=pl.ANY)
    vmem = pl.BlockSpec(memory_space=pltpu.VMEM)
    return pl.pallas_call(
        kernel,
        out_shape=(
            pltpu.VMEM((TOK, FB), BF16),
            pltpu.VMEM((OWN, FB), BF16),
        ),
        in_specs=[hbm, hbm, hbm, hbm],
        out_specs=(vmem, vmem),
        scratch_shapes=[
            pltpu.VMEM((2 * NX * NZ, ROWS, D), BF16),
            pltpu.VMEM((TOK, FB), BF16),
            pltpu.VMEM((FB, TOK), BF16),
            pltpu.VMEM((OWN, FB), BF16),
            pltpu.VMEM((OWN // QB, FB), BF16),
            pltpu.VMEM((8, OWN, FB), BF16),
            pltpu.VMEM((8, 2, FB, OWN // 2), BF16),
            pltpu.VMEM((2, 2, 2, FB, OWN // 2), BF16),
            pltpu.VMEM((2, 2, FB, OWN // 2), BF16),
            pltpu.VMEM((WS - 1, CW, 2, OWN // 2 // CW, FB), BF16),
            pltpu.VMEM((GS + 1, CG, 2, FB // CG, OWN // 2), BF16),
            pltpu.VMEM((2, FB, OWN // 2), F32),
            pltpu.VMEM((TOK, FB), F32),
            dma((4,)),
            dma((2,)), dma((NZ, FZ)),
            dma((1,)), dma((NZ,)), dma((1,)), dma((NZ,)),
            dma((1,)), dma((1,)),
            dma((1,)), dma((2, 2)), dma((1,)), dma((2,)),
            dma((1,)), dma((WS, CW)),
            dma((1,)), dma((2, CG)), dma((1,)), dma((2, CG)),
            dma((1,)), dma((GS, CG)),
        ],
        compiler_params=pltpu.CompilerParams(
            collective_id=0, has_side_effects=True, vmem_limit_bytes=56 << 20
        ),
        cost_estimate=pl.CostEstimate(
            flops=4 * TOK * D * FB, bytes_accessed=4 << 20, transcendentals=0
        ),
    )(hidden, cotangent, weight_codes, block_scales)


def solution(mesh):
    return jax.shard_map(
        body,
        mesh=mesh,
        in_specs=(
            P("node", "wide"),
            P(("node", "wide"), None),
            P("node", "wide"),
            P("node", "wide"),
        ),
        out_specs=(P("node", "wide"), P("node", "wide")),
        check_vma=False,
    )
```

```python
import functools

import jax
import jax.numpy as jnp
from jax import lax
from jax.experimental import pallas as pl
from jax.experimental.pallas import tpu as pltpu
from jax.sharding import PartitionSpec as P

MESH = pl.DeviceIdType.MESH
NX, NY, NZ = 4, 4, 8
D, FB, TOK, ROWS, QB = 4096, 384, 1024, 16, 128
OWN = D // 8
HALF = D // 2
FZ = 8
CW = 4
CG = 3
WH = 1
GH = 1
WS, GS = NZ // WH, NZ // GH
F32, BF16 = jnp.float32, jnp.bfloat16


def schedule():
    return [
        ("own",), ("weights",), ("z", 1, 0), ("z", 1, 1), ("z", 1, 2), ("z", 1, 3), ("z", 1, 4),
        ("z", 1, 5), ("z", 1, 6), ("z", 1, 7), ("w", 0, 0), ("z", 2, 0), ("z", 2, 1), ("z", 2, 2),
        ("z", 2, 3), ("z", 2, 4), ("z", 2, 5), ("z", 2, 6), ("z", 2, 7), ("xf", 0), ("z", 3, 0),
        ("z", 3, 1), ("z", 3, 2), ("w", 0, 1), ("z", 3, 3), ("z", 3, 4), ("z", 3, 5), ("z", 3, 6),
        ("z", 3, 7), ("z", 4, 0), ("z", 4, 1), ("z", 4, 2), ("z", 4, 3), ("z", 4, 4), ("z", 4, 5),
        ("z", 4, 6), ("z", 4, 7), ("w", 0, 2), ("z", 5, 0), ("xf", 1), ("z", 5, 1),
        ("near_weights",), ("z", 5, 2), ("z", 5, 3), ("z", 5, 4), ("z", 5, 5), ("w", 0, 3),
        ("z", 5, 6), ("z", 5, 7), ("z", 6, 0), ("z", 6, 1), ("w", 1, 0), ("z", 6, 2), ("turn",),
        ("z", 6, 3), ("z", 6, 4), ("xf", 2), ("z", 6, 5), ("xh", 0), ("z", 6, 6), ("w", 1, 1),
        ("z", 6, 7), ("z", 7, 0), ("z", 7, 1), ("w", 1, 2), ("z", 7, 2), ("near_halves",),
        ("xf", 3), ("w", 1, 3), ("z", 7, 3), ("z", 7, 4), ("w", 2, 0), ("z", 7, 5), ("z", 7, 6),
        ("xf", 4), ("w", 2, 1), ("z", 7, 7), ("w", 2, 2), ("w", 2, 3), ("w", 3, 0), ("xf", 5),
        ("w", 3, 1), ("xf", 6), ("w", 3, 2), ("w", 3, 3), ("xf", 7), ("xh", 1), ("w", 4, 0),
        ("xh", 3), ("w", 4, 1), ("w", 4, 2), ("xh", 2), ("xh", 6), ("xh", 4), ("xh", 5), ("xh", 7),
        ("w", 4, 3), ("w", 5, 0), ("w", 5, 1), ("cores",), ("term", 1, 2), ("gh", 1, 0),
        ("w", 5, 2), ("term", 1, 1), ("gh", 1, 2), ("w", 5, 3), ("w", 6, 0), ("gh", 1, 1),
        ("term", 1, -1), ("w", 6, 1), ("gn", 1, 0), ("w", 6, 2), ("term", 0, 1), ("w", 6, 3),
        ("term", 1, 0), ("w", 7, 0), ("gn", 1, 1), ("w", 7, 1), ("w", 7, 2), ("gn", 1, 2),
        ("term", 0, 2), ("gs", 0), ("w", 7, 3), ("hid", 0, 1), ("hid", 0, 0), ("gs", 1),
        ("term", 0, 0), ("g", 1, 0), ("gs", 2), ("g", 1, 1), ("far_weights",), ("g", 2, 0),
        ("hid", 0, 3), ("g", 1, 2), ("g", 2, 1), ("hid", 0, 2), ("gh", 0, 0), ("gh", 0, 1),
        ("g", 3, 0), ("g", 2, 2), ("term", 0, -1), ("g", 3, 1), ("g", 4, 0), ("g", 3, 2),
        ("gh", 0, 2), ("far_forward",), ("g", 4, 1), ("gn", 0, 1), ("g", 4, 2), ("gn", 0, 2),
        ("g", 5, 1), ("g", 5, 0), ("gn", 0, 0), ("g", 5, 2), ("g", 6, 1), ("far_halves",),
        ("g", 6, 0), ("hid", 1, 1), ("g", 6, 2), ("hid", 1, 2), ("ns", 1), ("g", 7, 1), ("g", 7, 0),
        ("ns", 2), ("g", 7, 2), ("hid", 1, 0), ("ns", 0), ("hid", 1, 3), ("left", 0), ("end", 0),
        ("end", 1), ("end", 2),
    ]


def kernel(
    hid_hbm, cot_hbm, codes_hbm, scales_hbm,
    hgrad_ref, wgrad_ref,
    cot, hid, hid_t, codes, scales, weight, part, ywhole, yhalf, wrelay, grelay, near_sum, hacc,
    local_sem, z_s, z_r, x_s, x_r, xh_s, xh_r, c_s, c_r,
    wy_s, wy_r, wh_s, wh_r, wz_s, wz_r, gy_s, gy_r, gh_s, gh_r, gz_s, gz_r,
):
    wide, node = lax.axis_index("wide"), lax.axis_index("node")
    x, zl, core = wide // (2 * NZ), (wide // 2) % NZ, wide % 2
    zh, y = node // NY, node % NY

    def at(dx=0, dy=0, dz=0):
        z = (zh * NZ + zl + dz + 2 * NZ) % (2 * NZ)
        return (
            ((x + dx + NX) % NX) * 2 * NZ + (z % NZ) * 2 + core,
            (z // NZ) * NY + (y + dy + NY) % NY,
        )

    sibling = (wide + 1 - 2 * core, node)
    ways_x = (at(dx=1), at(dx=-1))
    ways_y = (at(dy=1), at(dy=-1))
    ways_z = (at(dz=1), at(dz=-1))
    ways_w = (at(dz=WH), at(dz=-WH))
    ways_g = (at(dz=GH), at(dz=-GH))
    def remote(src, dst, s, r, to):
        return pltpu.make_async_remote_copy(
            src_ref=src, dst_ref=dst, send_sem=s, recv_sem=r, device_id=to, device_id_type=MESH
        )

    def send(src, dst, s, r, to):
        remote(src, dst, s, r, to).start()

    def landed(dst, r):
        remote(dst, dst, r, r, sibling).wait_recv()

    def left(src, s):
        remote(src, src, s, s, sibling).wait_send()

    def block(dx, z):
        return ((x + dx + NX) % NX) * 2 * NZ + z * 2 + core

    def near(dy):
        return zh * NY + (y + dy + NY) % NY

    def far(dy):
        return (1 - zh) * NY + (y + dy + NY) % NY

    def of(k, dy):
        return (near, far)[k](dy)


    fz = D // FZ

    def pass_on(z, f, d):
        piece = cot.at[block(0, z), :, pl.ds(f * fz, fz)]
        return remote(piece, piece, z_s.at[d], z_r.at[z, f], ways_z[d])

    def spread(z):
        b = block(0, z)
        for d in range(2):
            remote(cot.at[b], cot.at[b], x_s.at[0], x_r.at[z], ways_x[d]).start()
        remote(cot.at[b], cot.at[b], c_s.at[0], c_r.at[0], sibling).start()

    def go_own():
        for f in range(FZ):
            for d, inside in ((0, zl < NZ - 1), (1, zl > 0)):

                @pl.when(inside)
                def _():
                    pass_on(zl, f, d).start()

        spread(zl)

    def sides(s):
        return [(0, zl - s, zl - s >= 0), (1, zl + s, zl + s < NZ)][: 2 if s else 1]

    def go_z(s, f):
        for d, z, there in sides(s):

            @pl.when(there)
            def _():
                landed(cot.at[block(0, z), :, pl.ds(f * fz, fz)], z_r.at[z, f])

                @pl.when(zl < NZ - 1 if d == 0 else zl > 0)
                def _():
                    pass_on(z, f, d).start()

                if f == FZ - 1:
                    spread(z)

    def half_of(dx, z, d):
        return cot.at[block(dx, z), :, pl.ds(d * HALF, HALF)]

    def go_xf(s):
        for _, z, there in sides(s):

            @pl.when(there)
            def _():
                landed(cot.at[pl.ds(0, 2)], x_r.at[z])
                for d, dx in ((0, -1), (1, 1)):
                    half = half_of(dx, z, d)
                    send(half, half, xh_s.at[0], xh_r.at[z], ways_x[d])
                for dx in (-1, 1):
                    b = block(dx, z)
                    send(cot.at[b], cot.at[b], c_s.at[0], c_r.at[0], sibling)

    def go_xh(s):
        for _, z, there in sides(s):

            @pl.when(there)
            def _():
                b = block(2, z)
                landed(cot.at[b], xh_r.at[z])
                send(cot.at[b], cot.at[b], c_s.at[0], c_r.at[0], sibling)

    def go_cores():
        landed(cot.at[pl.ds(0, NX * NZ)], c_r.at[0])


    def weight_y(k):
        n = of(k, 0)
        for d in range(2):
            send(weight.at[n], weight.at[n], wy_s.at[0], wy_r.at[k, d], ways_y[d])

    def weight_forward(k):
        for d in range(2):
            n = of(k, -1 if d == 0 else 1)
            landed(weight.at[n], wy_r.at[k, d])
            half = weight.at[n, pl.ds(d * (OWN // 2), OWN // 2), :]
            send(half, half, wh_s.at[0], wh_r.at[k], ways_y[d])

    def weight_halves(k):
        landed(weight.at[of(k, 2)], wh_r.at[k])

    def go_weights():
        loads[1].wait()
        loads[3].wait()
        for q in range(OWN // QB):
            rows = pl.ds(q * QB, QB)
            weight[node, rows, :] = (
                codes[rows, :].astype(F32) * scales[pl.ds(q, 1), :].astype(F32)
            ).astype(BF16)
        weight_y(0)

    cw = OWN // 2 // CW

    def weight_piece(n, d, c):
        return weight.at[n, pl.ds(d * (OWN // 2) + c * cw, cw), :]

    def go_w(s, c):
        if s:
            landed(wrelay.at[s - 1, c], wz_r.at[s - 1, c])
        for d in range(2):
            src = weight_piece(node, d, c) if s == 0 else wrelay.at[s - 1, c, d]
            dst = wrelay.at[min(s, WS - 2), c, d]
            if s == WS - 1:
                z = zh * NZ + zl + (WH if d == 0 else -WH) + 2 * NZ
                dst = weight_piece((1 - (z // NZ) % 2) * NY + y, d, c)
            send(src, dst, wz_s.at[0], wz_r.at[s, c], ways_w[d])

    def go_far_weights():
        for c in range(CW):
            landed(wrelay.at[0, c], wz_r.at[WS - 1, c])
        weight_y(1)


    def go_turn():
        loads[2].wait()
        hid_t[...] = hid[...].T

    def go_term(k, dy):
        n = of(k, dy)

        @pl.loop(0, 2)
        def _(i):
            columns = pl.ds(pl.multiple_of(n * OWN + i * (OWN // 2), OWN // 2), OWN // 2)
            rows = cot[:, :, columns].reshape(TOK, OWN // 2)
            part[n, i] = jnp.dot(hid_t[...], rows, preferred_element_type=F32).astype(BF16)

    cg = FB // CG

    def units(c):
        return pl.ds(c * cg, cg)

    def go_gh(k, c):
        for d in range(2):
            send(
                part.at[of(k, 2), d, units(c), :], yhalf.at[k, d, units(c), :],
                gh_s.at[0], gh_r.at[k, c], ways_y[d],
            )

    def go_gn(k, c):
        landed(yhalf.at[k, :, units(c), :], gh_r.at[k, c])
        for d in range(2):
            n = of(k, 1 if d == 0 else -1)
            part[n, d, units(c), :] = (
                part[n, d, units(c), :].astype(F32) + yhalf[k, d, units(c), :].astype(F32)
            ).astype(BF16)
            send(
                part.at[n, :, units(c), :], ywhole.at[k, d, :, units(c), :],
                gy_s.at[0], gy_r.at[k, c], ways_y[d],
            )

    def summed(k, c):
        landed(ywhole.at[k, :, :, units(c), :], gy_r.at[k, c])
        return (
            part[of(k, 0), :, units(c), :].astype(F32)
            + ywhole[k, 0, :, units(c), :].astype(F32)
            + ywhole[k, 1, :, units(c), :].astype(F32)
        )

    def go_gs(c):
        grelay[0, c] = summed(1, c).astype(BF16)
        go_g(0, c)

    def go_g(s, c):
        if s:
            landed(grelay.at[s, c], gz_r.at[s - 1, c])
        for d in range(2):
            send(
                grelay.at[s, c, d], grelay.at[s + 1, c, d], gz_s.at[0], gz_r.at[s, c], ways_g[d]
            )

    def go_ns(c):
        near_sum[:, units(c), :] = summed(0, c)

    def go_end(c):
        landed(grelay.at[GS, c], gz_r.at[GS - 1, c])
        for d in range(2):
            total = near_sum[d, units(c), :] + grelay[GS, c, d].astype(F32)
            wgrad_ref[pl.ds(d * (OWN // 2), OWN // 2), units(c)] = (
                (total * float(TOK * 8) ** -0.5).T.astype(BF16)
            )


    def go_hid(k, i):
        rows = pl.ds(i * 256, 256)
        group = zh if k == 0 else 1 - zh
        features = pl.ds(pl.multiple_of(group * HALF, HALF), HALF)
        product = jnp.dot(
            cot[pl.ds(i * 16, 16), :, features].reshape(256, HALF),
            weight[pl.ds(group * NY, NY)].reshape(HALF, FB),
            preferred_element_type=F32,
        )
        if k == 0:
            hacc[rows, :] = product
        else:
            hgrad_ref[rows, :] = (hacc[rows, :] + product).astype(BF16)

    def go_left(k):
        if k:
            left(grelay.at[pl.ds(0, GS)], gz_s.at[0])
            return
        left(cot.at[pl.ds(0, 2 * NZ)], x_s.at[0])
        left(cot.at[pl.ds(0, NZ)], xh_s.at[0])
        left(cot.at[pl.ds(0, NX * NZ)], c_s.at[0])
        for z in range(1, NZ):

            @pl.when(zl == z - 1)
            def _():
                left(cot.at[pl.ds(0, z)], z_s.at[0])

            @pl.when(zl == NZ - z)
            def _():
                left(cot.at[pl.ds(0, z)], z_s.at[1])

        left(weight.at[pl.ds(0, 4)], wy_s.at[0])
        left(weight.at[pl.ds(0, 2)], wh_s.at[0])
        left(weight.at[pl.ds(0, WS)], wz_s.at[0])
        left(part.at[pl.ds(0, 2)], gh_s.at[0])
        left(part.at[pl.ds(0, 4)], gy_s.at[0])

    barrier = pltpu.get_barrier_semaphore()
    peers = [*ways_x, *ways_y, *ways_z, sibling]
    for hop in sorted({WH, GH} - {1}):
        peers += (at(dz=hop), at(dz=-hop))
    for peer in peers:
        pl.semaphore_signal(barrier, inc=1, device_id=peer, device_id_type=MESH)
    loads = [
        pltpu.make_async_copy(cot_hbm, cot.at[wide], local_sem.at[0]),
        pltpu.make_async_copy(codes_hbm, codes, local_sem.at[1]),
        pltpu.make_async_copy(hid_hbm, hid, local_sem.at[2]),
        pltpu.make_async_copy(scales_hbm, scales, local_sem.at[3]),
    ]
    for load in loads:
        load.start()
    loads[0].wait()
    pl.semaphore_wait(barrier, len(peers))

    steps = {
        "own": go_own, "weights": go_weights, "z": go_z, "xf": go_xf, "xh": go_xh, "cores": go_cores,
        "near_weights": functools.partial(weight_forward, 0), "turn": go_turn, "w": go_w,
        "far_weights": go_far_weights, "far_forward": functools.partial(weight_forward, 1),
        "near_halves": functools.partial(weight_halves, 0),
        "far_halves": functools.partial(weight_halves, 1),
        "term": go_term, "gh": go_gh, "gn": go_gn, "gs": go_gs, "g": go_g, "ns": go_ns,
        "hid": go_hid, "end": go_end, "left": go_left,
    }
    for name, *where in schedule():
        steps[name](*where)

    go_left(1)


def body(hidden, cotangent, weight_codes, block_scales):
    dma = pltpu.SemaphoreType.DMA
    hbm = pl.BlockSpec(memory_space=pl.ANY)
    vmem = pl.BlockSpec(memory_space=pltpu.VMEM)
    return pl.pallas_call(
        kernel,
        out_shape=(
            pltpu.VMEM((TOK, FB), BF16),
            pltpu.VMEM((OWN, FB), BF16),
        ),
        in_specs=[hbm, hbm, hbm, hbm],
        out_specs=(vmem, vmem),
        scratch_shapes=[
            pltpu.VMEM((2 * NX * NZ, ROWS, D), BF16),
            pltpu.VMEM((TOK, FB), BF16),
            pltpu.VMEM((FB, TOK), BF16),
            pltpu.VMEM((OWN, FB), BF16),
            pltpu.VMEM((OWN // QB, FB), BF16),
            pltpu.VMEM((8, OWN, FB), BF16),
            pltpu.VMEM((8, 2, FB, OWN // 2), BF16),
            pltpu.VMEM((2, 2, 2, FB, OWN // 2), BF16),
            pltpu.VMEM((2, 2, FB, OWN // 2), BF16),
            pltpu.VMEM((WS - 1, CW, 2, OWN // 2 // CW, FB), BF16),
            pltpu.VMEM((GS + 1, CG, 2, FB // CG, OWN // 2), BF16),
            pltpu.VMEM((2, FB, OWN // 2), F32),
            pltpu.VMEM((TOK, FB), F32),
            dma((4,)),
            dma((2,)), dma((NZ, FZ)),
            dma((1,)), dma((NZ,)), dma((1,)), dma((NZ,)),
            dma((1,)), dma((1,)),
            dma((1,)), dma((2, 2)), dma((1,)), dma((2,)),
            dma((1,)), dma((WS, CW)),
            dma((1,)), dma((2, CG)), dma((1,)), dma((2, CG)),
            dma((1,)), dma((GS, CG)),
        ],
        compiler_params=pltpu.CompilerParams(
            collective_id=0, has_side_effects=True, vmem_limit_bytes=56 << 20
        ),
        cost_estimate=pl.CostEstimate(
            flops=4 * TOK * D * FB, bytes_accessed=4 << 20, transcendentals=0
        ),
    )(hidden, cotangent, weight_codes, block_scales)


def solution(mesh):
    return jax.shard_map(
        body,
        mesh=mesh,
        in_specs=(
            P("node", "wide"),
            P(("node", "wide"), None),
            P("node", "wide"),
            P("node", "wide"),
        ),
        out_specs=(P("node", "wide"), P("node", "wide")),
        check_vma=False,
    )
```
